32 devices in a mesh: group: 2 (over x), dp: 16 (over z, y, core).
Axes of the slice: x: 2, y: 2, z: 4, core: 2. Of those that a mesh axis runs over, the one named last changes fastest.
Arguments:
- tokens: bfloat16 [4096, 8192], P(('group', 'dp')), parts along dimension 0, may hold values from -6 to 6
- grad_out: bfloat16 [4096, 8192], P(('group', 'dp')), parts along dimension 0, may hold values from -6 to 6
- down_factor_pool: bfloat16 [128, 8192, 128], P('group', 'dp'), parts along dimension 0, may hold values from -0.0625 to 0.0625
- up_pool: bfloat16 [128, 128, 8192], P('group', None, 'dp'), parts along dimension 0, may hold values from -0.25 to 0.25
- block_adapter: int32 [32], P('group'), parts along dimension 0, may hold values from 0 to 63, as said below
- counts: int32 [128], P('group'), parts along dimension 0, may hold values from 0 to 1024, as said below
- slot_map: int32 [128], P('group'), parts along dimension 0, may hold values from 0 to 63, each once
Outputs:
- adapter_output: bfloat16 [4096, 8192], P(('group', 'dp')), parts along dimension 0
- token_input_gradient: bfloat16 [4096, 8192], P(('group', 'dp')), parts along dimension 0
- down_factor_gradient: bfloat16 [128, 8192, 128], P('group', 'dp'), parts along dimension 0
- up_factor_gradient: bfloat16 [128, 128, 8192], P('group', None, 'dp'), parts along dimension 0
The draws below stay inside these ranges and needn't reach their ends.
There are 2 independent parts, one for each index of `group`. The reference program is written for one: setup_inputs(seed, part) draws one part's arguments, and reference() takes and returns one part's arrays. A program takes and returns all parts, laid end to end along the dimension named above; each array names one. Nothing has to cross between parts.
Inputs may be any that keep to these rules, and one draw needn't show every extreme that they name: `block_adapter`: some block names adapter 0 and some adapter 64 - 1; no adapter is named by more than 8 blocks. `counts`: an adapter with k listed blocks has more than 128 * (k - 1) and at most 128 * k tokens; one with none has 0. `slot_map`: a permutation.
All inputs are finite; a program needn't handle non-finite values.
Results may differ from the reference program's by a relative error of at most 0.005.
Values may be sent and summed in bfloat16 or wider, within the bound.
A program may use at most 128 MiB of HBM per device.

```python
import jax
import jax.numpy as jnp
from jax import lax

MODEL_WIDTH = 8192
R = 128
ADAPTERS = 64
BLOCK = 128
BLOCKS = 16
TOKEN_ROWS_ALL = 2048


def shared_blocks(key):
    keys = jax.random.split(key, 4)
    order = jax.random.permutation(keys[0], BLOCKS)
    heavy_mask = order < BLOCKS // 2
    first_draw = jax.random.randint(keys[1], (BLOCKS,), 0, ADAPTERS - 1)
    second_draw = jax.random.randint(keys[2], (BLOCKS,), 0, ADAPTERS - 1)
    relabel = jax.random.permutation(keys[3], ADAPTERS - 1)
    adapter_ids = relabel[jnp.minimum(first_draw, second_draw)]
    adapter_ids = jnp.where(order == BLOCKS // 2, 0, adapter_ids)
    adapter_ids = jnp.where(heavy_mask, ADAPTERS - 1, adapter_ids)
    return adapter_ids.astype(jnp.int32)


def draw_block_adapter(key, part):
    adapter_ids = shared_blocks(key)
    return adapter_ids


def draw_counts(key, part):
    adapter_ids = shared_blocks(key)
    key = jax.random.fold_in(key, 7)
    matches = adapter_ids[:, None] == jnp.arange(ADAPTERS)[None, :]
    held = jnp.sum(matches.astype(jnp.int32), axis=0)
    last_fill = jax.random.randint(key, (ADAPTERS,), 1, BLOCK + 1)
    last_fill = jnp.where(jnp.arange(ADAPTERS) == ADAPTERS - 1, BLOCK, last_fill)
    return jnp.where(held > 0, BLOCK * (held - 1) + last_fill, 0).astype(jnp.int32)


def strengthened(values, stream_key, source, target, blocks, factor):
    def block_of(axis_at):
        return (jnp.arange(values.shape[axis_at]) // (values.shape[axis_at] // blocks)).reshape((-1,) + (1,) * (values.ndim - 1 - axis_at))

    near = jax.random.permutation(stream_key, blocks)[block_of(target)]
    second = (block_of(target) + blocks // 2) % blocks
    return jnp.where((block_of(source) == near) | (block_of(source) == second), factor * values, values)


def block_scale(own_key, dims, shards, least, top_value):
    gain, own = 1.0, jax.random.fold_in(own_key, 6)
    for axis_at, blocks in shards:
        heights = jnp.exp(jax.random.uniform(jax.random.fold_in(own, axis_at), (blocks,), jnp.float32, least / len(shards), top_value / len(shards)))
        gain = gain * jnp.repeat(heights, dims[axis_at] // blocks).reshape([-1 if axis == axis_at else 1 for axis in range(len(dims))])
    return gain


def centred(stream_key, dims, spread, reach, cuts=(), held_as=jnp.bfloat16):
    entries = jax.random.normal(stream_key, dims, jnp.float32) * spread
    if len(cuts) > 0:
        entries = block_scale(stream_key, dims, cuts, -0.22, 0.18) * entries
    return jnp.clip(entries, min=-reach, max=reach).astype(held_as)


def heavy_noise(stream_key, shape, deviation, reach, pieces, heavy, kind=jnp.bfloat16):
    entries = deviation * jax.random.normal(stream_key, shape, jnp.float32)
    if pieces:
        entries = entries * block_scale(stream_key, shape, pieces, -0.22, 0.18)
    return jnp.clip(strengthened(entries, jax.random.fold_in(stream_key, 3), *heavy), -reach, reach).astype(kind)


def setup_inputs(seed: int = 0, part: int = 0) -> dict:
    key_of = jax.random.split(jax.random.key(seed), 8)
    part_keys = jax.random.split(jax.random.fold_in(key_of[7], part), 8)
    tokens = heavy_noise(part_keys[0], (TOKEN_ROWS_ALL, MODEL_WIDTH), 1.0, 6.0, ((0, 16),), (1, 0, 16, 2.0))
    grad_out = centred(part_keys[1], (TOKEN_ROWS_ALL, MODEL_WIDTH), 1.0, 6.0, ((0, 16),))
    down_factor_pool = centred(part_keys[2], (ADAPTERS, MODEL_WIDTH, R), MODEL_WIDTH ** -0.5, 0.0625, ((1, 16),))
    up_pool = centred(part_keys[3], (ADAPTERS, R, MODEL_WIDTH), (4 * R) ** -0.5, 0.25, ((2, 16),))
    block_adapter = draw_block_adapter(jax.random.fold_in(jax.random.fold_in(key_of[7], part), 71), part)
    counts = draw_counts(jax.random.fold_in(jax.random.fold_in(key_of[7], part), 71), part)
    slot_map = jax.random.permutation(part_keys[6], ADAPTERS).astype(jnp.int32)
    return dict(tokens=tokens, grad_out=grad_out, down_factor_pool=down_factor_pool, up_pool=up_pool, block_adapter=block_adapter, counts=counts, slot_map=slot_map)


adapter_scale = 2.0


def block_tables(block_adapter, counts, slot_map, rows_per_block):
    blocks = block_adapter.shape[0]
    adapter_list = counts.shape[0]
    matches = block_adapter[:, None] == jnp.arange(adapter_list, dtype=jnp.int32)[None, :]
    block_count = jnp.sum(jnp.where(matches, counts[None, :], 0), axis=1)
    block_position = jnp.sum(jnp.where(matches, slot_map[None, :], 0), axis=1).astype(jnp.int32)
    same_adapter = block_adapter[:, None] == block_adapter[None, :]
    position = jnp.arange(blocks, dtype=jnp.int32)
    before = position[None, :] < position[:, None]
    ordinal = jnp.sum((same_adapter & before).astype(jnp.int32), axis=1)
    live_rows = jnp.clip(block_count - rows_per_block * ordinal, 0, rows_per_block).astype(jnp.int32)
    holder = slot_map[:, None] == jnp.arange(adapter_list, dtype=jnp.int32)[None, :]
    slot_count = jnp.sum(jnp.where(holder, counts[:, None], 0), axis=0).astype(jnp.int32)
    return block_position, live_rows, slot_count


def reference(tokens, grad_out, down_factor_pool, up_pool, block_adapter, counts, slot_map):
    block_position, live_rows, slot_count = block_tables(block_adapter, counts, slot_map, BLOCK)
    active_row_mask = (jnp.arange(BLOCK, dtype=jnp.int32)[None, :] < live_rows[:, None]).astype(jnp.float32)
    input_rows = tokens.reshape(BLOCKS, BLOCK, MODEL_WIDTH)
    gradient_rows = grad_out.reshape(BLOCKS, BLOCK, MODEL_WIDTH)

    def block_stride(totals, inputs):
        gradient_down_part, gradient_up_part = totals
        x_block, gradient_block, slot_id, active_row = inputs
        down_block = lax.dynamic_index_in_dim(down_factor_pool, slot_id, 0, keepdims=False)
        up_factor_block = lax.dynamic_index_in_dim(up_pool, slot_id, 0, keepdims=False)
        reduced_state = (jnp.dot(x_block, down_block, preferred_element_type=jnp.float32) * active_row[:, None]).astype(jnp.bfloat16)
        block_result = (adapter_scale * jnp.dot(reduced_state, up_factor_block, preferred_element_type=jnp.float32)).astype(jnp.bfloat16)
        reduced_gradient = (adapter_scale * active_row[:, None] * jnp.dot(gradient_block, up_factor_block.T, preferred_element_type=jnp.float32)).astype(jnp.bfloat16)
        incoming_gradient = jnp.dot(reduced_gradient, down_block.T, preferred_element_type=jnp.float32).astype(jnp.bfloat16)
        term_a = jnp.dot(x_block.T, reduced_gradient, preferred_element_type=jnp.float32)
        second_term = adapter_scale * jnp.dot(reduced_state.T, gradient_block, preferred_element_type=jnp.float32)
        gradient_down_part = lax.dynamic_update_index_in_dim(gradient_down_part, lax.dynamic_index_in_dim(gradient_down_part, slot_id, 0, keepdims=False) + term_a, slot_id, 0)
        gradient_up_part = lax.dynamic_update_index_in_dim(gradient_up_part, lax.dynamic_index_in_dim(gradient_up_part, slot_id, 0, keepdims=False) + second_term, slot_id, 0)
        return (gradient_down_part, gradient_up_part), (block_result, incoming_gradient)

    starting_totals = (jnp.zeros((ADAPTERS, MODEL_WIDTH, R), jnp.float32), jnp.zeros((ADAPTERS, R, MODEL_WIDTH), jnp.float32))
    (gradient_down_part, gradient_up_part), (adapter_output, token_input_gradient) = lax.scan(block_stride, starting_totals, (input_rows, gradient_rows, block_position, active_row_mask))
    inverse = 1.0 / jnp.maximum(slot_count, 1).astype(jnp.float32)
    down_factor_gradient = (gradient_down_part * inverse[:, None, None]).astype(jnp.bfloat16)
    up_factor_gradient = (gradient_up_part * inverse[:, None, None]).astype(jnp.bfloat16)
    return adapter_output.reshape(TOKEN_ROWS_ALL, MODEL_WIDTH), token_input_gradient.reshape(TOKEN_ROWS_ALL, MODEL_WIDTH), down_factor_gradient, up_factor_gradient
```

```python
import functools

import jax
import jax.numpy as jnp
from jax import lax
from jax.experimental import pallas as pl
from jax.experimental.pallas import tpu as pltpu
from jax.sharding import PartitionSpec as P

BLOCK = 128


adapter_scale = 2.0


def block_tables(block_adapter, counts, slot_map, rows_per_block):
    blocks = block_adapter.shape[0]
    adapter_list = counts.shape[0]
    matches = block_adapter[:, None] == jnp.arange(adapter_list, dtype=jnp.int32)[None, :]
    block_count = jnp.sum(jnp.where(matches, counts[None, :], 0), axis=1)
    block_position = jnp.sum(jnp.where(matches, slot_map[None, :], 0), axis=1)
    same_adapter = block_adapter[:, None] == block_adapter[None, :]
    position = jnp.arange(blocks, dtype=jnp.int32)
    before = position[None, :] < position[:, None]
    ordinal = jnp.sum((same_adapter & before).astype(jnp.int32), axis=1)
    live_rows = jnp.clip(block_count - rows_per_block * ordinal, 0, rows_per_block)
    holder = slot_map[:, None] == jnp.arange(adapter_list, dtype=jnp.int32)[None, :]
    slot_count = jnp.sum(jnp.where(holder, counts[:, None], 0), axis=0)
    return (block_position, live_rows, slot_count)


def per_slot(chooser, pieces):
    blocks = pieces.shape[0]
    summed = jnp.dot(
        chooser,
        pieces.reshape(blocks, -1),
        precision=lax.Precision.HIGHEST,
        preferred_element_type=jnp.float32,
    )
    return summed.reshape((chooser.shape[0],) + pieces.shape[1:])


def collective_body(tokens, grad_out, down_factor_pool, up_pool, block_adapter, counts, slot_map):
    token_per_device, model_width = tokens.shape
    rows_per_block = BLOCK
    block_per_device = token_per_device // rows_per_block
    adapter_list, segment_width, adapter_rank = down_factor_pool.shape
    block_position, live_rows, slot_count = block_tables(
        block_adapter, counts, slot_map, rows_per_block
    )
    first_block = lax.axis_index("dp") * block_per_device
    own_live = lax.dynamic_slice_in_dim(live_rows, first_block, block_per_device)
    active_row_mask = (
        (jnp.arange(rows_per_block, dtype=jnp.int32)[None, :] < own_live[:, None])
        .astype(jnp.float32)
        .reshape(token_per_device, 1)
    )
    columns = None
    columns = lax.all_to_all(tokens, "dp", split_axis=1, concat_axis=0, tiled=True)
    down_sel = down_factor_pool[block_position]
    up_turned = jnp.swapaxes(up_pool, 1, 2)
    up_sel = up_turned[block_position]
    down_full, up_full = (
        lax.all_to_all(down_sel, "dp", split_axis=0, concat_axis=1, tiled=True),
        lax.all_to_all(up_sel, "dp", split_axis=0, concat_axis=1, tiled=True),
    )
    x_blocks = tokens.reshape(block_per_device, rows_per_block, model_width)
    count_of_rows = token_per_device * lax.axis_size("dp")
    token_slab = columns.reshape(count_of_rows // rows_per_block, rows_per_block, segment_width)
    summed_low = lax.psum_scatter(
        jnp.einsum(
            "kbd,kdr->kbr", token_slab, down_sel, preferred_element_type=jnp.float32
        ).reshape(count_of_rows, adapter_rank),
        "dp",
        scatter_dimension=0,
        tiled=True,
    )
    projected_rows = (summed_low * active_row_mask).astype(jnp.bfloat16)
    reduced_blocks = projected_rows.reshape(block_per_device, rows_per_block, adapter_rank)
    adapter_output = (
        (
            adapter_scale
            * jnp.einsum(
                "kbr,kdr->kbd", reduced_blocks, up_full, preferred_element_type=jnp.float32
            )
        )
        .astype(jnp.bfloat16)
        .reshape(token_per_device, model_width)
    )
    g_blocks = grad_out.reshape(block_per_device, rows_per_block, model_width)
    backward_total = jnp.einsum(
        "kbd,kdr->kbr", g_blocks, up_full, preferred_element_type=jnp.float32
    ).reshape(token_per_device, adapter_rank)
    reduced_gradient = (adapter_scale * active_row_mask * backward_total).astype(jnp.bfloat16)
    gradient_block_list = reduced_gradient.reshape(block_per_device, rows_per_block, adapter_rank)
    chooser = (
        jnp.arange(adapter_list, dtype=jnp.int32)[:, None] == block_position[None, :]
    ).astype(jnp.float32)
    inverse = 1.0 / jnp.maximum(slot_count, 1).astype(jnp.float32)
    sum_b = None
    second_term = None
    second_term = adapter_scale * jnp.einsum(
        "kbd,kbr->kdr", g_blocks, reduced_blocks, preferred_element_type=jnp.float32
    )
    incoming_gradient = (
        jnp.einsum(
            "kbr,kdr->kbd", gradient_block_list, down_full, preferred_element_type=jnp.float32
        )
        .astype(jnp.bfloat16)
        .reshape(token_per_device, model_width)
    )
    term_a = jnp.einsum(
        "kbd,kbr->kdr", x_blocks, gradient_block_list, preferred_element_type=jnp.float32
    )
    got_a, got_b = (
        lax.all_to_all(term_a, "dp", split_axis=1, concat_axis=0, tiled=True),
        lax.all_to_all(second_term, "dp", split_axis=1, concat_axis=0, tiled=True),
    )
    sum_b = per_slot(chooser, got_b)
    sum_a = per_slot(chooser, got_a)
    down_factor_gradient = (sum_a * inverse[:, None, None]).astype(jnp.bfloat16)
    up_factor_gradient = jnp.swapaxes(sum_b * inverse[:, None, None], 1, 2).astype(jnp.bfloat16)
    return (adapter_output, incoming_gradient, down_factor_gradient, up_factor_gradient)


VMEM_BYTES = 48 * 1024 * 1024


def pick_kernel(blocks, slots, down_pool, up_pool, down_sel, up_sel, sems):
    def copies(k):
        return (
            pltpu.make_async_copy(down_pool.at[slots[k]], down_sel.at[k], sems.at[0, k]),
            pltpu.make_async_copy(up_pool.at[slots[k]], up_sel.at[k], sems.at[1, k]),
        )

    @pl.loop(0, blocks)
    def _(k):
        for copy in copies(k):
            copy.start()

    @pl.loop(0, blocks)
    def _(k):
        for copy in copies(k):
            copy.wait()


def pick(block_position, down_pool, up_pool):
    blocks = block_position.shape[0]
    any_spec = pl.BlockSpec(memory_space=pl.ANY)
    return pl.pallas_call(
        functools.partial(pick_kernel, blocks),
        grid_spec=pltpu.PrefetchScalarGridSpec(
            num_scalar_prefetch=1,
            grid=(1,),
            in_specs=[any_spec] * 2,
            out_specs=[any_spec] * 2,
            scratch_shapes=[pltpu.SemaphoreType.DMA((2, blocks))],
        ),
        out_shape=[
            jax.ShapeDtypeStruct((blocks,) + down_pool.shape[1:], jnp.bfloat16),
            jax.ShapeDtypeStruct((blocks,) + up_pool.shape[1:], jnp.bfloat16),
        ],
        name="pick_factors",
    )(block_position, down_pool, up_pool)


def exchange_kernel(
    n, seg,
    tok, grd, down_sel, up_sel, mask,
    out, tig, x_slab, g_slab, packs,
    tok_v, grd_v, down_v, up_v, low_acc, grad_acc, mine, out_v, tig_v,
    send, recv, own_send, fwd_send, pack_recv, local,
):
    me = lax.axis_index("dp")
    half = n // 2
    rows = mask.shape[0]
    partner = lax.rem(me + half, n)
    base = (me // half) * half

    def columns(j):
        return pl.ds(pl.multiple_of(j * seg, 128), seg)

    def source(a, j):
        if a == 0:
            return down_sel.at[j]
        if a == 1:
            return up_sel.at[j]
        return (tok if a == 2 else grd).at[:, columns(j)]

    landing = (down_v, up_v, x_slab, g_slab)

    def outgoing(a, peer):
        return pltpu.make_async_remote_copy(
            src_ref=source(a, peer), dst_ref=landing[a].at[me],
            send_sem=send.at[a, peer], recv_sem=recv.at[a, me],
            device_id={"dp": peer}, device_id_type=pl.DeviceIdType.MESH,
        )

    def incoming(a, j):
        return pltpu.make_async_remote_copy(
            src_ref=source(a, j), dst_ref=landing[a].at[j],
            send_sem=send.at[a, j], recv_sem=recv.at[a, j],
            device_id={"dp": j}, device_id_type=pl.DeviceIdType.MESH,
        )

    def own_pack(peer, origin):
        return pltpu.make_async_remote_copy(
            src_ref=mine, dst_ref=packs.at[origin],
            send_sem=own_send.at[peer], recv_sem=pack_recv.at[origin],
            device_id={"dp": peer}, device_id_type=pl.DeviceIdType.MESH,
        )

    def forwarded(peer):
        return pltpu.make_async_remote_copy(
            src_ref=packs.at[partner], dst_ref=packs.at[partner],
            send_sem=fwd_send.at[peer], recv_sem=pack_recv.at[partner],
            device_id={"dp": peer}, device_id_type=pl.DeviceIdType.MESH,
        )

    def near(d):
        return base + lax.rem(me - base + d, half)

    barrier = pltpu.get_barrier_semaphore()

    @pl.loop(1, n)
    def _(d):
        pl.semaphore_signal(
            barrier, inc=1, device_id={"dp": lax.rem(me + d, n)},
            device_id_type=pl.DeviceIdType.MESH,
        )

    pl.semaphore_wait(barrier, n - 1)

    @pl.loop(1, n)
    def _(d):
        peer = lax.rem(me + d, n)
        outgoing(0, peer).start()
        outgoing(1, peer).start()

    @pl.loop(1, n)
    def _(d):
        outgoing(2, lax.rem(me + d, n)).start()

    first = [
        pltpu.make_async_copy(tok, tok_v, local.at[0]),
        pltpu.make_async_copy(grd, grd_v, local.at[1]),
        pltpu.make_async_copy(down_sel.at[me], down_v.at[me], local.at[2]),
        pltpu.make_async_copy(up_sel.at[me], up_v.at[me], local.at[3]),
    ]
    later = [
        pltpu.make_async_copy(tok.at[:, columns(me)], x_slab.at[me], local.at[4]),
        pltpu.make_async_copy(grd.at[:, columns(me)], g_slab.at[me], local.at[5]),
    ]
    for copy in first + later:
        copy.start()
    for copy in first:
        copy.wait()
    low_acc[...] = jnp.zeros_like(low_acc)
    grad_acc[...] = jnp.zeros_like(grad_acc)

    def contract(j):
        cols = columns(j)
        low_acc[...] += jnp.dot(tok_v[:, cols], down_v[j], preferred_element_type=jnp.float32)
        grad_acc[...] += lax.dot_general(
            grd_v[:, cols], up_v[j], (((1,), (1,)), ((), ())),
            preferred_element_type=jnp.float32,
        )

    contract(me)

    @pl.loop(1, n)
    def _(d):
        j = lax.rem(me - d + n, n)
        incoming(0, j).wait_recv()
        incoming(1, j).wait_recv()
        contract(j)

    mine[:rows, :] = (low_acc[...] * mask[...]).astype(jnp.bfloat16)
    mine[rows:, :] = (adapter_scale * mask[...] * grad_acc[...]).astype(jnp.bfloat16)
    own = pltpu.make_async_copy(mine, packs.at[me], local.at[6])
    own.start()
    own_pack(partner, me).start()

    @pl.loop(1, half)
    def _(d):
        own_pack(near(d), me).start()

    @pl.loop(1, n)
    def _(d):
        outgoing(3, lax.rem(me + d, n)).start()

    @pl.loop(0, n)
    def _(j):
        cols = columns(j)
        out_v[:, cols] = (
            adapter_scale
            * jnp.dot(mine[:rows, :], up_v[j], preferred_element_type=jnp.float32)
        ).astype(jnp.bfloat16)
        tig_v[:, cols] = lax.dot_general(
            mine[rows:, :], down_v[j], (((1,), (1,)), ((), ())),
            preferred_element_type=jnp.float32,
        ).astype(jnp.bfloat16)

    results = [
        pltpu.make_async_copy(out_v, out, local.at[7]),
        pltpu.make_async_copy(tig_v, tig, local.at[8]),
    ]
    for copy in results:
        copy.start()
    own_pack(partner, partner).wait_recv()

    @pl.loop(1, half)
    def _(d):
        forwarded(near(d)).start()

    @pl.loop(1, half)
    def _(d):
        peer = near(d)
        own_pack(peer, peer).wait_recv()
        own_pack(peer, lax.rem(peer + half, n)).wait_recv()

    for copy in later + [own] + results:
        copy.wait()

    @pl.loop(1, half)
    def _(d):
        own_pack(near(d), me).wait_send()
        forwarded(near(d)).wait_send()

    own_pack(partner, me).wait_send()

    @pl.loop(1, n)
    def _(d):
        peer = lax.rem(me + d, n)
        for a in range(4):
            outgoing(a, peer).wait_send()
        incoming(2, peer).wait_recv()
        incoming(3, peer).wait_recv()


def exchange(n, tokens, grad_out, down_sel, up_sel, mask):
    rows, width = tokens.shape
    seg, rank = down_sel.shape[1:]
    any_spec = pl.BlockSpec(memory_space=pl.ANY)
    sems = pltpu.SemaphoreType.DMA
    bf16, f32 = jnp.bfloat16, jnp.float32
    return pl.pallas_call(
        functools.partial(exchange_kernel, n, seg),
        in_specs=[any_spec] * 4 + [pl.BlockSpec(memory_space=pltpu.VMEM)],
        out_specs=[any_spec] * 5,
        out_shape=[
            jax.ShapeDtypeStruct((rows, width), bf16),
            jax.ShapeDtypeStruct((rows, width), bf16),
            jax.ShapeDtypeStruct((n, rows, seg), bf16),
            jax.ShapeDtypeStruct((n, rows, seg), bf16),
            jax.ShapeDtypeStruct((n, 2 * rows, rank), bf16),
        ],
        scratch_shapes=[
            pltpu.VMEM((rows, width), bf16),
            pltpu.VMEM((rows, width), bf16),
            pltpu.VMEM((n, seg, rank), bf16),
            pltpu.VMEM((n, rank, seg), bf16),
            pltpu.VMEM((rows, rank), f32),
            pltpu.VMEM((rows, rank), f32),
            pltpu.VMEM((2 * rows, rank), bf16),
            pltpu.VMEM((rows, width), bf16),
            pltpu.VMEM((rows, width), bf16),
            sems((4, n)),
            sems((4, n)),
            sems((n,)),
            sems((n,)),
            sems((n,)),
            sems((9,)),
        ],
        compiler_params=pltpu.CompilerParams(
            collective_id=0, has_side_effects=True, vmem_limit_bytes=VMEM_BYTES
        ),
        name="exchange",
    )(tokens, grad_out, down_sel, up_sel, mask)


def factor_kernel(per_step, order, start, inverse, x_slab, g_slab, packs, down_grad, up_grad):
    rows = x_slab.shape[1]
    first = pl.program_id(0) * per_step

    @pl.loop(0, per_step)
    def _(i):
        slot = first + i
        down_grad[i] = jnp.zeros(down_grad.shape[1:], down_grad.dtype)
        up_grad[i] = jnp.zeros(up_grad.shape[1:], up_grad.dtype)
        begin, end = start[slot], start[slot + 1]

        @pl.when(end > begin)
        def _():
            def terms(position):
                k = order[position]
                pack = packs[k]
                over_rows = (((0,), (0,)), ((), ()))
                term_a = lax.dot_general(
                    x_slab[k], pack[rows:], over_rows, preferred_element_type=jnp.float32
                )
                term_b = lax.dot_general(
                    pack[:rows], g_slab[k], over_rows, preferred_element_type=jnp.float32
                )
                return term_a, term_b

            def add(position, totals):
                term_a, term_b = terms(position)
                return totals[0] + term_a, totals[1] + term_b

            total_a, total_b = lax.fori_loop(begin + 1, end, add, terms(begin))
            scale = inverse[slot]
            down_grad[i] = (total_a * scale).astype(down_grad.dtype)
            up_grad[i] = (adapter_scale * total_b * scale).astype(up_grad.dtype)


def factor_gradients(order, start, inverse, x_slab, g_slab, packs):
    slots = inverse.shape[0]
    _, rows, seg = x_slab.shape
    rank = packs.shape[2]
    per_step = 4 if slots % 4 == 0 else 1
    whole = pl.BlockSpec(memory_space=pltpu.VMEM)
    return pl.pallas_call(
        functools.partial(factor_kernel, per_step),
        grid_spec=pltpu.PrefetchScalarGridSpec(
            num_scalar_prefetch=3,
            grid=(slots // per_step,),
            in_specs=[whole] * 3,
            out_specs=[
                pl.BlockSpec((per_step, seg, rank), lambda i, *_: (i, 0, 0)),
                pl.BlockSpec((per_step, rank, seg), lambda i, *_: (i, 0, 0)),
            ],
        ),
        out_shape=[
            jax.ShapeDtypeStruct((slots, seg, rank), jnp.bfloat16),
            jax.ShapeDtypeStruct((slots, rank, seg), jnp.bfloat16),
        ],
        compiler_params=pltpu.CompilerParams(vmem_limit_bytes=VMEM_BYTES),
        name="factor_gradients",
    )(order, start, inverse, x_slab, g_slab, packs)


def kernel_body(tokens, grad_out, down_factor_pool, up_pool, block_adapter, counts, slot_map):
    n = lax.axis_size("dp")
    slots, _, rank = down_factor_pool.shape
    block_position, live_rows, slot_count = block_tables(block_adapter, counts, slot_map, BLOCK)
    own_live = lax.dynamic_slice_in_dim(live_rows, lax.axis_index("dp"), 1)
    mask = (
        lax.broadcasted_iota(jnp.int32, (BLOCK, rank), 0) < own_live[:, None]
    ).astype(jnp.float32)
    down_sel, up_sel = pick(block_position, down_factor_pool, up_pool)
    out, tig, x_slab, g_slab, packs = exchange(n, tokens, grad_out, down_sel, up_sel, mask)
    index = jnp.arange(n, dtype=jnp.int32)
    keys = block_position * n + index
    rank_of = jnp.sum((keys[None, :] < keys[:, None]).astype(jnp.int32), axis=1)
    order = jnp.sum(jnp.where(rank_of[None, :] == index[:, None], index[None, :], 0), axis=1)
    slot_ids = jnp.arange(slots + 1, dtype=jnp.int32)
    start = jnp.sum((block_position[None, :] < slot_ids[:, None]).astype(jnp.int32), axis=1)
    inverse = 1.0 / jnp.maximum(slot_count, 1).astype(jnp.float32)
    down_grad, up_grad = factor_gradients(order, start, inverse, x_slab, g_slab, packs)
    return out, tig, down_grad, up_grad


def body(tokens, *rest):
    n = lax.axis_size("dp")
    seg = rest[1].shape[1]
    if tokens.shape[0] == BLOCK and seg % 128 == 0 and n % 2 == 0:
        return kernel_body(tokens, *rest)
    return collective_body(tokens, *rest)


def solution(mesh):
    placed = (
        P(("group", "dp"), None),
        P(("group", "dp"), None),
        P("group", "dp", None),
        P("group", None, "dp"),
        P("group"),
        P("group"),
        P("group"),
    )
    return jax.shard_map(
        body,
        mesh=mesh,
        in_specs=placed,
        out_specs=(
            P(("group", "dp"), None),
            P(("group", "dp"), None),
            P("group", "dp", None),
            P("group", None, "dp"),
        ),
        check_vma=False,
    )
```

```python
import functools

import jax
import jax.numpy as jnp
from jax import lax
from jax.experimental import pallas as pl
from jax.experimental.pallas import tpu as pltpu
from jax.sharding import PartitionSpec as P

BLOCK = 128


adapter_scale = 2.0


def block_tables(block_adapter, counts, slot_map, rows_per_block):
    blocks = block_adapter.shape[0]
    adapter_list = counts.shape[0]
    matches = block_adapter[:, None] == jnp.arange(adapter_list, dtype=jnp.int32)[None, :]
    block_count = jnp.sum(jnp.where(matches, counts[None, :], 0), axis=1)
    block_position = jnp.sum(jnp.where(matches, slot_map[None, :], 0), axis=1)
    same_adapter = block_adapter[:, None] == block_adapter[None, :]
    position = jnp.arange(blocks, dtype=jnp.int32)
    before = position[None, :] < position[:, None]
    ordinal = jnp.sum((same_adapter & before).astype(jnp.int32), axis=1)
    live_rows = jnp.clip(block_count - rows_per_block * ordinal, 0, rows_per_block)
    holder = slot_map[:, None] == jnp.arange(adapter_list, dtype=jnp.int32)[None, :]
    slot_count = jnp.sum(jnp.where(holder, counts[:, None], 0), axis=0)
    return (block_position, live_rows, slot_count)


def per_slot(chooser, pieces):
    blocks = pieces.shape[0]
    summed = jnp.dot(
        chooser,
        pieces.reshape(blocks, -1),
        precision=lax.Precision.HIGHEST,
        preferred_element_type=jnp.float32,
    )
    return summed.reshape((chooser.shape[0],) + pieces.shape[1:])


def collective_body(tokens, grad_out, down_factor_pool, up_pool, block_adapter, counts, slot_map):
    token_per_device, model_width = tokens.shape
    rows_per_block = BLOCK
    block_per_device = token_per_device // rows_per_block
    adapter_list, segment_width, adapter_rank = down_factor_pool.shape
    block_position, live_rows, slot_count = block_tables(
        block_adapter, counts, slot_map, rows_per_block
    )
    first_block = lax.axis_index("dp") * block_per_device
    own_live = lax.dynamic_slice_in_dim(live_rows, first_block, block_per_device)
    active_row_mask = (
        (jnp.arange(rows_per_block, dtype=jnp.int32)[None, :] < own_live[:, None])
        .astype(jnp.float32)
        .reshape(token_per_device, 1)
    )
    columns = None
    columns = lax.all_to_all(tokens, "dp", split_axis=1, concat_axis=0, tiled=True)
    down_sel = down_factor_pool[block_position]
    up_turned = jnp.swapaxes(up_pool, 1, 2)
    up_sel = up_turned[block_position]
    down_full, up_full = (
        lax.all_to_all(down_sel, "dp", split_axis=0, concat_axis=1, tiled=True),
        lax.all_to_all(up_sel, "dp", split_axis=0, concat_axis=1, tiled=True),
    )
    x_blocks = tokens.reshape(block_per_device, rows_per_block, model_width)
    count_of_rows = token_per_device * lax.axis_size("dp")
    token_slab = columns.reshape(count_of_rows // rows_per_block, rows_per_block, segment_width)
    summed_low = lax.psum_scatter(
        jnp.einsum(
            "kbd,kdr->kbr", token_slab, down_sel, preferred_element_type=jnp.float32
        ).reshape(count_of_rows, adapter_rank),
        "dp",
        scatter_dimension=0,
        tiled=True,
    )
    projected_rows = (summed_low * active_row_mask).astype(jnp.bfloat16)
    reduced_blocks = projected_rows.reshape(block_per_device, rows_per_block, adapter_rank)
    adapter_output = (
        (
            adapter_scale
            * jnp.einsum(
                "kbr,kdr->kbd", reduced_blocks, up_full, preferred_element_type=jnp.float32
            )
        )
        .astype(jnp.bfloat16)
        .reshape(token_per_device, model_width)
    )
    g_blocks = grad_out.reshape(block_per_device, rows_per_block, model_width)
    backward_total = jnp.einsum(
        "kbd,kdr->kbr", g_blocks, up_full, preferred_element_type=jnp.float32
    ).reshape(token_per_device, adapter_rank)
    reduced_gradient = (adapter_scale * active_row_mask * backward_total).astype(jnp.bfloat16)
    gradient_block_list = reduced_gradient.reshape(block_per_device, rows_per_block, adapter_rank)
    chooser = (
        jnp.arange(adapter_list, dtype=jnp.int32)[:, None] == block_position[None, :]
    ).astype(jnp.float32)
    inverse = 1.0 / jnp.maximum(slot_count, 1).astype(jnp.float32)
    sum_b = None
    second_term = None
    second_term = adapter_scale * jnp.einsum(
        "kbd,kbr->kdr", g_blocks, reduced_blocks, preferred_element_type=jnp.float32
    )
    incoming_gradient = (
        jnp.einsum(
            "kbr,kdr->kbd", gradient_block_list, down_full, preferred_element_type=jnp.float32
        )
        .astype(jnp.bfloat16)
        .reshape(token_per_device, model_width)
    )
    term_a = jnp.einsum(
        "kbd,kbr->kdr", x_blocks, gradient_block_list, preferred_element_type=jnp.float32
    )
    got_a, got_b = (
        lax.all_to_all(term_a, "dp", split_axis=1, concat_axis=0, tiled=True),
        lax.all_to_all(second_term, "dp", split_axis=1, concat_axis=0, tiled=True),
    )
    sum_b = per_slot(chooser, got_b)
    sum_a = per_slot(chooser, got_a)
    down_factor_gradient = (sum_a * inverse[:, None, None]).astype(jnp.bfloat16)
    up_factor_gradient = jnp.swapaxes(sum_b * inverse[:, None, None], 1, 2).astype(jnp.bfloat16)
    return (adapter_output, incoming_gradient, down_factor_gradient, up_factor_gradient)


MIB = 1024 * 1024


def pick_kernel(
    n, slots,
    block_adapter, counts, slot_map, down_pool, up_pool,
    down_sel, up_sel, mask, order, start,
    held, ordinal, get,
):
    def slot_of(k):
        return slot_map[block_adapter[k]]

    def gets(k):
        return (
            pltpu.make_async_copy(down_pool.at[slot_of(k)], down_sel.at[k], get.at[0, k]),
            pltpu.make_async_copy(up_pool.at[slot_of(k)], up_sel.at[k], get.at[1, k]),
        )

    @pl.loop(0, n)
    def _(k):
        for copy in gets(k):
            copy.start()

    @pl.loop(0, slots)
    def _(s):
        held[s] = 0

    @pl.loop(0, n)
    def _(k):
        s = slot_of(k)
        ordinal[k] = held[s]
        held[s] = held[s] + 1

    start[0] = 0

    @pl.loop(0, slots)
    def _(s):
        start[s + 1] = start[s] + held[s]

    @pl.loop(0, n)
    def _(k):
        order[start[slot_of(k)] + ordinal[k]] = k

    me = lax.axis_index("dp")
    rows = mask.shape[0]
    live = counts[block_adapter[me]] - rows * ordinal[me]
    row = lax.broadcasted_iota(jnp.int32, mask.shape, 0)
    mask[...] = jnp.where(row < live, 1.0, 0.0).astype(jnp.float32)

    @pl.loop(0, n)
    def _(k):
        for copy in gets(k):
            copy.wait()


def pick(block_adapter, counts, slot_map, down_pool, up_pool):
    n = block_adapter.shape[0]
    slots, seg, rank = down_pool.shape
    hbm = pl.BlockSpec(memory_space=pltpu.HBM)
    vmem = pl.BlockSpec(memory_space=pltpu.VMEM)
    smem = pl.BlockSpec(memory_space=pltpu.SMEM)
    return pl.pallas_call(
        functools.partial(pick_kernel, n, slots),
        in_specs=[smem] * 3 + [hbm] * 2,
        out_specs=[vmem] * 3 + [smem] * 2,
        out_shape=[
            jax.ShapeDtypeStruct((n, seg, rank), jnp.bfloat16),
            jax.ShapeDtypeStruct((n, rank, seg), jnp.bfloat16),
            jax.ShapeDtypeStruct((BLOCK, rank), jnp.float32),
            jax.ShapeDtypeStruct((n,), jnp.int32),
            jax.ShapeDtypeStruct((slots + 1,), jnp.int32),
        ],
        scratch_shapes=[
            pltpu.SMEM((slots,), jnp.int32),
            pltpu.SMEM((n,), jnp.int32),
            pltpu.SemaphoreType.DMA((2, n)),
        ],
        compiler_params=pltpu.CompilerParams(vmem_limit_bytes=8 * MIB),
        name="pick_factors",
    )(block_adapter, counts, slot_map, down_pool, up_pool)


def exchange_kernel(
    n, seg,
    tok, grd, down_sel, up_sel, mask,
    out, tig, x_slab, g_slab, packs,
    tok_v, grd_v, down_v, up_v, low_acc, grad_acc, mine,
    send, recv, own_send, fwd_send, pack_recv, local,
):
    me = lax.axis_index("dp")
    half = n // 2
    rows = mask.shape[0]
    partner = lax.rem(me + half, n)
    base = (me // half) * half

    def columns(j):
        return pl.ds(pl.multiple_of(j * seg, 128), seg)

    def source(a, j):
        if a == 0:
            return down_sel.at[j]
        if a == 1:
            return up_sel.at[j]
        return (tok if a == 2 else grd).at[:, columns(j)]

    landing = (down_v, up_v, x_slab, g_slab)

    def outgoing(a, peer):
        return pltpu.make_async_remote_copy(
            src_ref=source(a, peer), dst_ref=landing[a].at[me],
            send_sem=send.at[a, peer], recv_sem=recv.at[a, me],
            device_id={"dp": peer}, device_id_type=pl.DeviceIdType.MESH,
        )

    def incoming(a, j):
        return pltpu.make_async_remote_copy(
            src_ref=source(a, j), dst_ref=landing[a].at[j],
            send_sem=send.at[a, j], recv_sem=recv.at[a, j],
            device_id={"dp": j}, device_id_type=pl.DeviceIdType.MESH,
        )

    def own_pack(peer, origin):
        return pltpu.make_async_remote_copy(
            src_ref=mine, dst_ref=packs.at[origin],
            send_sem=own_send.at[peer], recv_sem=pack_recv.at[origin],
            device_id={"dp": peer}, device_id_type=pl.DeviceIdType.MESH,
        )

    def forwarded(peer):
        return pltpu.make_async_remote_copy(
            src_ref=packs.at[partner], dst_ref=packs.at[partner],
            send_sem=fwd_send.at[peer], recv_sem=pack_recv.at[partner],
            device_id={"dp": peer}, device_id_type=pl.DeviceIdType.MESH,
        )

    def near(d):
        return base + lax.rem(me - base + d, half)

    barrier = pltpu.get_barrier_semaphore()

    @pl.loop(1, n)
    def _(d):
        pl.semaphore_signal(
            barrier, inc=1, device_id={"dp": lax.rem(me + d, n)},
            device_id_type=pl.DeviceIdType.MESH,
        )

    pl.semaphore_wait(barrier, n - 1)

    @pl.loop(1, n)
    def _(d):
        peer = lax.rem(me + d, n)
        outgoing(0, peer).start()
        outgoing(1, peer).start()

    @pl.loop(1, n)
    def _(d):
        outgoing(2, lax.rem(me + d, n)).start()

    first = [
        pltpu.make_async_copy(tok, tok_v, local.at[0]),
        pltpu.make_async_copy(grd, grd_v, local.at[1]),
        pltpu.make_async_copy(down_sel.at[me], down_v.at[me], local.at[2]),
        pltpu.make_async_copy(up_sel.at[me], up_v.at[me], local.at[3]),
    ]
    later = [
        pltpu.make_async_copy(tok.at[:, columns(me)], x_slab.at[me], local.at[4]),
        pltpu.make_async_copy(grd.at[:, columns(me)], g_slab.at[me], local.at[5]),
    ]
    for copy in first + later:
        copy.start()
    for copy in first:
        copy.wait()
    low_acc[...] = jnp.zeros_like(low_acc)
    grad_acc[...] = jnp.zeros_like(grad_acc)

    def contract(j):
        cols = columns(j)
        low_acc[...] += jnp.dot(tok_v[:, cols], down_v[j], preferred_element_type=jnp.float32)
        grad_acc[...] += lax.dot_general(
            grd_v[:, cols], up_v[j], (((1,), (1,)), ((), ())),
            preferred_element_type=jnp.float32,
        )

    contract(me)

    @pl.loop(1, n)
    def _(d):
        j = lax.rem(me - d + n, n)
        incoming(0, j).wait_recv()
        incoming(1, j).wait_recv()
        contract(j)

    mine[:rows, :] = (low_acc[...] * mask[...]).astype(jnp.bfloat16)
    mine[rows:, :] = (adapter_scale * mask[...] * grad_acc[...]).astype(jnp.bfloat16)
    own = pltpu.make_async_copy(mine, packs.at[me], local.at[6])
    own.start()
    own_pack(partner, me).start()

    @pl.loop(1, half)
    def _(d):
        own_pack(near(d), me).start()

    @pl.loop(1, n)
    def _(d):
        outgoing(3, lax.rem(me + d, n)).start()

    @pl.loop(0, n)
    def _(j):
        cols = columns(j)
        out[:, cols] = (
            adapter_scale
            * jnp.dot(mine[:rows, :], up_v[j], preferred_element_type=jnp.float32)
        ).astype(jnp.bfloat16)
        tig[:, cols] = lax.dot_general(
            mine[rows:, :], down_v[j], (((1,), (1,)), ((), ())),
            preferred_element_type=jnp.float32,
        ).astype(jnp.bfloat16)

    own_pack(partner, partner).wait_recv()

    @pl.loop(1, half)
    def _(d):
        forwarded(near(d)).start()

    @pl.loop(1, half)
    def _(d):
        peer = near(d)
        own_pack(peer, peer).wait_recv()
        own_pack(peer, lax.rem(peer + half, n)).wait_recv()

    for copy in later + [own]:
        copy.wait()

    @pl.loop(1, half)
    def _(d):
        own_pack(near(d), me).wait_send()
        forwarded(near(d)).wait_send()

    own_pack(partner, me).wait_send()

    @pl.loop(1, n)
    def _(d):
        peer = lax.rem(me + d, n)
        for a in range(4):
            outgoing(a, peer).wait_send()
        incoming(2, peer).wait_recv()
        incoming(3, peer).wait_recv()


def exchange(n, tokens, grad_out, down_sel, up_sel, mask):
    rows, width = tokens.shape
    seg, rank = down_sel.shape[1:]
    hbm = pl.BlockSpec(memory_space=pltpu.HBM)
    vmem = pl.BlockSpec(memory_space=pltpu.VMEM)
    sems = pltpu.SemaphoreType.DMA
    bf16, f32 = jnp.bfloat16, jnp.float32
    return pl.pallas_call(
        functools.partial(exchange_kernel, n, seg),
        in_specs=[hbm] * 2 + [vmem] * 3,
        out_specs=[vmem] * 2 + [vmem] * 3,
        out_shape=[
            jax.ShapeDtypeStruct((rows, width), bf16),
            jax.ShapeDtypeStruct((rows, width), bf16),
            jax.ShapeDtypeStruct((n, rows, seg), bf16),
            jax.ShapeDtypeStruct((n, rows, seg), bf16),
            jax.ShapeDtypeStruct((n, 2 * rows, rank), bf16),
        ],
        scratch_shapes=[
            pltpu.VMEM((rows, width), bf16),
            pltpu.VMEM((rows, width), bf16),
            pltpu.VMEM((n, seg, rank), bf16),
            pltpu.VMEM((n, rank, seg), bf16),
            pltpu.VMEM((rows, rank), f32),
            pltpu.VMEM((rows, rank), f32),
            pltpu.VMEM((2 * rows, rank), bf16),
            sems((4, n)),
            sems((4, n)),
            sems((n,)),
            sems((n,)),
            sems((n,)),
            sems((7,)),
        ],
        compiler_params=pltpu.CompilerParams(
            collective_id=0, has_side_effects=True, vmem_limit_bytes=16 * MIB
        ),
        name="exchange",
    )(tokens, grad_out, down_sel, up_sel, mask)


def factor_kernel(
    n, slots,
    block_adapter, counts, slot_map, order, start, x_slab, g_slab, packs, out_in, tig_in,
    out, tig, down_grad, up_grad,
    no_down, no_up, acc_a, acc_b, sum_a, sum_b,
    put, put_out,
):
    rows = x_slab.shape[1]

    def puts(slot, down_ref, up_ref):
        return (
            pltpu.make_async_copy(down_ref, down_grad.at[slot], put.at[0, slot]),
            pltpu.make_async_copy(up_ref, up_grad.at[slot], put.at[1, slot]),
        )

    out_puts = (
        pltpu.make_async_copy(out_in, out, put_out.at[0]),
        pltpu.make_async_copy(tig_in, tig, put_out.at[1]),
    )

    for copy in out_puts:
        copy.start()
    no_down[...] = jnp.zeros_like(no_down)
    no_up[...] = jnp.zeros_like(no_up)

    @pl.loop(0, slots)
    def _(slot):
        @pl.when(start[slot] == start[slot + 1])
        def _():
            for copy in puts(slot, no_down, no_up):
                copy.start()

    @pl.loop(0, n)
    def _(i):
        k = order[i]
        slot = slot_map[block_adapter[k]]
        over_rows = (((0,), (0,)), ((), ()))
        term_a = lax.dot_general(
            x_slab[k], packs[k, rows:, :], over_rows, preferred_element_type=jnp.float32
        )
        term_b = lax.dot_general(
            packs[k, :rows, :], g_slab[k], over_rows, preferred_element_type=jnp.float32
        )
        fresh = i == start[slot]
        acc_a[...] = jnp.where(fresh, term_a, acc_a[...] + term_a)
        acc_b[...] = jnp.where(fresh, term_b, acc_b[...] + term_b)

        @pl.when(i + 1 == start[slot + 1])
        def _():
            held = jnp.maximum(counts[block_adapter[k]], 1)
            scale = 1.0 / jnp.full((1, 128), held, jnp.int32).astype(jnp.float32)
            sum_a[i] = (acc_a[...] * scale[:, :1]).astype(jnp.bfloat16)
            sum_b[i] = (adapter_scale * acc_b[...] * scale[:, :1]).astype(jnp.bfloat16)
            for copy in puts(slot, sum_a.at[i], sum_b.at[i]):
                copy.start()

    for copy in out_puts:
        copy.wait()

    @pl.loop(0, slots)
    def _(slot):
        for copy in puts(slot, no_down, no_up):
            copy.wait()


def factor_gradients(block_adapter, counts, slot_map, order, start, x_slab, g_slab, packs, out, tig):
    slots = slot_map.shape[0]
    n, rows, seg = x_slab.shape
    rank = packs.shape[2]
    hbm = pl.BlockSpec(memory_space=pltpu.HBM)
    vmem = pl.BlockSpec(memory_space=pltpu.VMEM)
    smem = pl.BlockSpec(memory_space=pltpu.SMEM)
    bf16, f32 = jnp.bfloat16, jnp.float32
    sems = pltpu.SemaphoreType.DMA
    return pl.pallas_call(
        functools.partial(factor_kernel, n, slots),
        in_specs=[smem] * 5 + [vmem] * 3 + [vmem] * 2,
        out_specs=[hbm] * 4,
        out_shape=[
            jax.ShapeDtypeStruct(out.shape, bf16),
            jax.ShapeDtypeStruct(tig.shape, bf16),
            jax.ShapeDtypeStruct((slots, seg, rank), bf16),
            jax.ShapeDtypeStruct((slots, rank, seg), bf16),
        ],
        scratch_shapes=[
            pltpu.VMEM((seg, rank), bf16),
            pltpu.VMEM((rank, seg), bf16),
            pltpu.VMEM((seg, rank), f32),
            pltpu.VMEM((rank, seg), f32),
            pltpu.VMEM((n, seg, rank), bf16),
            pltpu.VMEM((n, rank, seg), bf16),
            sems((2, slots)),
            sems((2,)),
        ],
        compiler_params=pltpu.CompilerParams(vmem_limit_bytes=24 * MIB),
        name="factor_gradients",
    )(block_adapter, counts, slot_map, order, start, x_slab, g_slab, packs, out, tig)


def kernel_body(tokens, grad_out, down_factor_pool, up_pool, *tables):
    n = lax.axis_size("dp")
    down_sel, up_sel, mask, order, start = pick(*tables, down_factor_pool, up_pool)
    out, tig, x_slab, g_slab, packs = exchange(n, tokens, grad_out, down_sel, up_sel, mask)
    return factor_gradients(*tables, order, start, x_slab, g_slab, packs, out, tig)


def body(tokens, *rest):
    n = lax.axis_size("dp")
    seg = rest[1].shape[1]
    if tokens.shape[0] == BLOCK and seg % 128 == 0 and n % 2 == 0:
        return kernel_body(tokens, *rest)
    return collective_body(tokens, *rest)


def solution(mesh):
    placed = (
        P(("group", "dp"), None),
        P(("group", "dp"), None),
        P("group", "dp", None),
        P("group", None, "dp"),
        P("group"),
        P("group"),
        P("group"),
    )
    return jax.shard_map(
        body,
        mesh=mesh,
        in_specs=placed,
        out_specs=(
            P(("group", "dp"), None),
            P(("group", "dp"), None),
            P("group", "dp", None),
            P("group", None, "dp"),
        ),
        check_vma=False,
    )
```

```python
import functools

import jax
import jax.numpy as jnp
from jax import lax
from jax.experimental import pallas as pl
from jax.experimental.pallas import tpu as pltpu
from jax.sharding import PartitionSpec as P

BLOCK = 128


adapter_scale = 2.0


def block_tables(block_adapter, counts, slot_map, rows_per_block):
    blocks = block_adapter.shape[0]
    adapter_list = counts.shape[0]
    matches = block_adapter[:, None] == jnp.arange(adapter_list, dtype=jnp.int32)[None, :]
    block_count = jnp.sum(jnp.where(matches, counts[None, :], 0), axis=1)
    block_position = jnp.sum(jnp.where(matches, slot_map[None, :], 0), axis=1)
    same_adapter = block_adapter[:, None] == block_adapter[None, :]
    position = jnp.arange(blocks, dtype=jnp.int32)
    before = position[None, :] < position[:, None]
    ordinal = jnp.sum((same_adapter & before).astype(jnp.int32), axis=1)
    live_rows = jnp.clip(block_count - rows_per_block * ordinal, 0, rows_per_block)
    holder = slot_map[:, None] == jnp.arange(adapter_list, dtype=jnp.int32)[None, :]
    slot_count = jnp.sum(jnp.where(holder, counts[:, None], 0), axis=0)
    return (block_position, live_rows, slot_count)


def per_slot(chooser, pieces):
    blocks = pieces.shape[0]
    summed = jnp.dot(
        chooser,
        pieces.reshape(blocks, -1),
        precision=lax.Precision.HIGHEST,
        preferred_element_type=jnp.float32,
    )
    return summed.reshape((chooser.shape[0],) + pieces.shape[1:])


def collective_body(tokens, grad_out, down_factor_pool, up_pool, block_adapter, counts, slot_map):
    token_per_device, model_width = tokens.shape
    rows_per_block = BLOCK
    block_per_device = token_per_device // rows_per_block
    adapter_list, segment_width, adapter_rank = down_factor_pool.shape
    block_position, live_rows, slot_count = block_tables(
        block_adapter, counts, slot_map, rows_per_block
    )
    first_block = lax.axis_index("dp") * block_per_device
    own_live = lax.dynamic_slice_in_dim(live_rows, first_block, block_per_device)
    active_row_mask = (
        (jnp.arange(rows_per_block, dtype=jnp.int32)[None, :] < own_live[:, None])
        .astype(jnp.float32)
        .reshape(token_per_device, 1)
    )
    columns = None
    columns = lax.all_to_all(tokens, "dp", split_axis=1, concat_axis=0, tiled=True)
    down_sel = down_factor_pool[block_position]
    up_turned = jnp.swapaxes(up_pool, 1, 2)
    up_sel = up_turned[block_position]
    down_full, up_full = (
        lax.all_to_all(down_sel, "dp", split_axis=0, concat_axis=1, tiled=True),
        lax.all_to_all(up_sel, "dp", split_axis=0, concat_axis=1, tiled=True),
    )
    x_blocks = tokens.reshape(block_per_device, rows_per_block, model_width)
    count_of_rows = token_per_device * lax.axis_size("dp")
    token_slab = columns.reshape(count_of_rows // rows_per_block, rows_per_block, segment_width)
    summed_low = lax.psum_scatter(
        jnp.einsum(
            "kbd,kdr->kbr", token_slab, down_sel, preferred_element_type=jnp.float32
        ).reshape(count_of_rows, adapter_rank),
        "dp",
        scatter_dimension=0,
        tiled=True,
    )
    projected_rows = (summed_low * active_row_mask).astype(jnp.bfloat16)
    reduced_blocks = projected_rows.reshape(block_per_device, rows_per_block, adapter_rank)
    adapter_output = (
        (
            adapter_scale
            * jnp.einsum(
                "kbr,kdr->kbd", reduced_blocks, up_full, preferred_element_type=jnp.float32
            )
        )
        .astype(jnp.bfloat16)
        .reshape(token_per_device, model_width)
    )
    g_blocks = grad_out.reshape(block_per_device, rows_per_block, model_width)
    backward_total = jnp.einsum(
        "kbd,kdr->kbr", g_blocks, up_full, preferred_element_type=jnp.float32
    ).reshape(token_per_device, adapter_rank)
    reduced_gradient = (adapter_scale * active_row_mask * backward_total).astype(jnp.bfloat16)
    gradient_block_list = reduced_gradient.reshape(block_per_device, rows_per_block, adapter_rank)
    chooser = (
        jnp.arange(adapter_list, dtype=jnp.int32)[:, None] == block_position[None, :]
    ).astype(jnp.float32)
    inverse = 1.0 / jnp.maximum(slot_count, 1).astype(jnp.float32)
    sum_b = None
    second_term = None
    second_term = adapter_scale * jnp.einsum(
        "kbd,kbr->kdr", g_blocks, reduced_blocks, preferred_element_type=jnp.float32
    )
    incoming_gradient = (
        jnp.einsum(
            "kbr,kdr->kbd", gradient_block_list, down_full, preferred_element_type=jnp.float32
        )
        .astype(jnp.bfloat16)
        .reshape(token_per_device, model_width)
    )
    term_a = jnp.einsum(
        "kbd,kbr->kdr", x_blocks, gradient_block_list, preferred_element_type=jnp.float32
    )
    got_a, got_b = (
        lax.all_to_all(term_a, "dp", split_axis=1, concat_axis=0, tiled=True),
        lax.all_to_all(second_term, "dp", split_axis=1, concat_axis=0, tiled=True),
    )
    sum_b = per_slot(chooser, got_b)
    sum_a = per_slot(chooser, got_a)
    down_factor_gradient = (sum_a * inverse[:, None, None]).astype(jnp.bfloat16)
    up_factor_gradient = jnp.swapaxes(sum_b * inverse[:, None, None], 1, 2).astype(jnp.bfloat16)
    return (adapter_output, incoming_gradient, down_factor_gradient, up_factor_gradient)


MIB = 1024 * 1024


def pick_kernel(
    n, slots,
    block_adapter, counts, slot_map, down_pool, up_pool,
    down_sel, up_sel, mask, order, start,
    held, ordinal, get,
):
    def slot_of(k):
        return slot_map[block_adapter[k]]

    def gets(k):
        return (
            pltpu.make_async_copy(down_pool.at[slot_of(k)], down_sel.at[k], get.at[0, k]),
            pltpu.make_async_copy(up_pool.at[slot_of(k)], up_sel.at[k], get.at[1, k]),
        )

    @pl.loop(0, n)
    def _(k):
        for copy in gets(k):
            copy.start()

    @pl.loop(0, slots)
    def _(s):
        held[s] = 0

    @pl.loop(0, n)
    def _(k):
        s = slot_of(k)
        ordinal[k] = held[s]
        held[s] = held[s] + 1

    start[0] = 0

    @pl.loop(0, slots)
    def _(s):
        start[s + 1] = start[s] + held[s]

    @pl.loop(0, n)
    def _(k):
        order[start[slot_of(k)] + ordinal[k]] = k

    me = lax.axis_index("dp")
    rows = mask.shape[0]
    live = counts[block_adapter[me]] - rows * ordinal[me]
    row = lax.broadcasted_iota(jnp.int32, mask.shape, 0)
    mask[...] = jnp.where(row < live, 1.0, 0.0).astype(jnp.float32)

    @pl.loop(0, n)
    def _(k):
        for copy in gets(k):
            copy.wait()


def pick(block_adapter, counts, slot_map, down_pool, up_pool):
    n = block_adapter.shape[0]
    slots, seg, rank = down_pool.shape
    hbm = pl.BlockSpec(memory_space=pltpu.HBM)
    vmem = pl.BlockSpec(memory_space=pltpu.VMEM)
    smem = pl.BlockSpec(memory_space=pltpu.SMEM)
    return pl.pallas_call(
        functools.partial(pick_kernel, n, slots),
        in_specs=[smem] * 3 + [hbm] * 2,
        out_specs=[vmem] * 3 + [smem] * 2,
        out_shape=[
            jax.ShapeDtypeStruct((n, seg, rank), jnp.bfloat16),
            jax.ShapeDtypeStruct((n, rank, seg), jnp.bfloat16),
            jax.ShapeDtypeStruct((BLOCK, rank), jnp.float32),
            jax.ShapeDtypeStruct((n,), jnp.int32),
            jax.ShapeDtypeStruct((slots + 1,), jnp.int32),
        ],
        scratch_shapes=[
            pltpu.SMEM((slots,), jnp.int32),
            pltpu.SMEM((n,), jnp.int32),
            pltpu.SemaphoreType.DMA((2, n)),
        ],
        compiler_params=pltpu.CompilerParams(vmem_limit_bytes=54 * MIB),
        name="pick_factors",
    )(block_adapter, counts, slot_map, down_pool, up_pool)


def exchange_kernel(
    n, seg,
    tok, grd, down_sel, up_sel, mask,
    out, tig, x_slab, g_slab, packs,
    tok_v, grd_v, down_v, up_v, low_acc, grad_acc, mine,
    send, recv, own_send, fwd_send, pack_recv, local,
):
    me = lax.axis_index("dp")
    half = n // 2
    rows = mask.shape[0]
    partner = lax.rem(me + half, n)
    base = (me // half) * half

    def columns(j):
        return pl.ds(pl.multiple_of(j * seg, 128), seg)

    def source(a, j):
        if a == 0:
            return down_sel.at[j]
        if a == 1:
            return up_sel.at[j]
        return (tok if a == 2 else grd).at[:, columns(j)]

    landing = (down_v, up_v, x_slab, g_slab)

    def outgoing(a, peer):
        return pltpu.make_async_remote_copy(
            src_ref=source(a, peer), dst_ref=landing[a].at[me],
            send_sem=send.at[a, peer], recv_sem=recv.at[a, me],
            device_id={"dp": peer}, device_id_type=pl.DeviceIdType.MESH,
        )

    def incoming(a, j):
        return pltpu.make_async_remote_copy(
            src_ref=source(a, j), dst_ref=landing[a].at[j],
            send_sem=send.at[a, j], recv_sem=recv.at[a, j],
            device_id={"dp": j}, device_id_type=pl.DeviceIdType.MESH,
        )

    def own_pack(peer, origin):
        return pltpu.make_async_remote_copy(
            src_ref=mine, dst_ref=packs.at[origin],
            send_sem=own_send.at[peer], recv_sem=pack_recv.at[origin],
            device_id={"dp": peer}, device_id_type=pl.DeviceIdType.MESH,
        )

    def forwarded(peer):
        return pltpu.make_async_remote_copy(
            src_ref=packs.at[partner], dst_ref=packs.at[partner],
            send_sem=fwd_send.at[peer], recv_sem=pack_recv.at[partner],
            device_id={"dp": peer}, device_id_type=pl.DeviceIdType.MESH,
        )

    def near(d):
        return base + lax.rem(me - base + d, half)

    barrier = pltpu.get_barrier_semaphore()

    @pl.loop(1, n)
    def _(d):
        pl.semaphore_signal(
            barrier, inc=1, device_id={"dp": lax.rem(me + d, n)},
            device_id_type=pl.DeviceIdType.MESH,
        )

    pl.semaphore_wait(barrier, n - 1)

    @pl.loop(1, n)
    def _(d):
        outgoing(0, lax.rem(me + d, n)).start()

    @pl.loop(1, n)
    def _(d):
        outgoing(1, lax.rem(me + d, n)).start()

    @pl.loop(1, n)
    def _(d):
        outgoing(2, lax.rem(me + d, n)).start()

    first = [
        pltpu.make_async_copy(tok, tok_v, local.at[0]),
        pltpu.make_async_copy(grd, grd_v, local.at[1]),
        pltpu.make_async_copy(down_sel.at[me], down_v.at[me], local.at[2]),
        pltpu.make_async_copy(up_sel.at[me], up_v.at[me], local.at[3]),
    ]
    later = [
        pltpu.make_async_copy(tok.at[:, columns(me)], x_slab.at[me], local.at[4]),
        pltpu.make_async_copy(grd.at[:, columns(me)], g_slab.at[me], local.at[5]),
    ]
    for copy in first + later:
        copy.start()
    for copy in first:
        copy.wait()
    low_acc[...] = jnp.zeros_like(low_acc)
    grad_acc[...] = jnp.zeros_like(grad_acc)

    def contract(j):
        cols = columns(j)
        low_acc[...] += jnp.dot(tok_v[:, cols], down_v[j], preferred_element_type=jnp.float32)
        grad_acc[...] += lax.dot_general(
            grd_v[:, cols], up_v[j], (((1,), (1,)), ((), ())),
            preferred_element_type=jnp.float32,
        )

    contract(me)

    @pl.loop(1, n)
    def _(d):
        j = lax.rem(me - d + n, n)
        incoming(0, j).wait_recv()
        incoming(1, j).wait_recv()
        contract(j)

    mine[:rows, :] = (low_acc[...] * mask[...]).astype(jnp.bfloat16)
    mine[rows:, :] = (adapter_scale * mask[...] * grad_acc[...]).astype(jnp.bfloat16)
    own = pltpu.make_async_copy(mine, packs.at[me], local.at[6])
    own.start()
    own_pack(partner, me).start()

    @pl.loop(1, half)
    def _(d):
        own_pack(near(d), me).start()

    @pl.loop(1, n)
    def _(d):
        outgoing(3, lax.rem(me + d, n)).start()

    @pl.loop(0, n)
    def _(j):
        cols = columns(j)
        out[:, cols] = (
            adapter_scale
            * jnp.dot(mine[:rows, :], up_v[j], preferred_element_type=jnp.float32)
        ).astype(jnp.bfloat16)
        tig[:, cols] = lax.dot_general(
            mine[rows:, :], down_v[j], (((1,), (1,)), ((), ())),
            preferred_element_type=jnp.float32,
        ).astype(jnp.bfloat16)

    own_pack(partner, partner).wait_recv()

    @pl.loop(1, half)
    def _(d):
        forwarded(near(d)).start()

    @pl.loop(1, half)
    def _(d):
        peer = near(d)
        own_pack(peer, peer).wait_recv()
        own_pack(peer, lax.rem(peer + half, n)).wait_recv()

    for copy in later + [own]:
        copy.wait()

    @pl.loop(1, half)
    def _(d):
        own_pack(near(d), me).wait_send()
        forwarded(near(d)).wait_send()

    own_pack(partner, me).wait_send()

    @pl.loop(1, n)
    def _(d):
        peer = lax.rem(me + d, n)
        for a in range(4):
            outgoing(a, peer).wait_send()
        incoming(2, peer).wait_recv()
        incoming(3, peer).wait_recv()


def exchange(n, tokens, grad_out, down_sel, up_sel, mask):
    rows, width = tokens.shape
    seg, rank = down_sel.shape[1:]
    hbm = pl.BlockSpec(memory_space=pltpu.HBM)
    vmem = pl.BlockSpec(memory_space=pltpu.VMEM)
    sems = pltpu.SemaphoreType.DMA
    bf16, f32 = jnp.bfloat16, jnp.float32
    return pl.pallas_call(
        functools.partial(exchange_kernel, n, seg),
        in_specs=[hbm] * 2 + [vmem] * 3,
        out_specs=[vmem] * 2 + [vmem] * 3,
        out_shape=[
            jax.ShapeDtypeStruct((rows, width), bf16),
            jax.ShapeDtypeStruct((rows, width), bf16),
            jax.ShapeDtypeStruct((n, rows, seg), bf16),
            jax.ShapeDtypeStruct((n, rows, seg), bf16),
            jax.ShapeDtypeStruct((n, 2 * rows, rank), bf16),
        ],
        scratch_shapes=[
            pltpu.VMEM((rows, width), bf16),
            pltpu.VMEM((rows, width), bf16),
            pltpu.VMEM((n, seg, rank), bf16),
            pltpu.VMEM((n, rank, seg), bf16),
            pltpu.VMEM((rows, rank), f32),
            pltpu.VMEM((rows, rank), f32),
            pltpu.VMEM((2 * rows, rank), bf16),
            sems((4, n)),
            sems((4, n)),
            sems((n,)),
            sems((n,)),
            sems((n,)),
            sems((7,)),
        ],
        compiler_params=pltpu.CompilerParams(
            collective_id=0, has_side_effects=True, vmem_limit_bytes=16 * MIB
        ),
        name="exchange",
    )(tokens, grad_out, down_sel, up_sel, mask)


def factor_kernel(
    n, slots,
    block_adapter, counts, slot_map, order, start, x_slab, g_slab, packs, out_in, tig_in,
    out, tig, down_grad, up_grad,
    no_down, no_up, acc_a, acc_b, sum_a, sum_b,
    put, put_out,
):
    rows = x_slab.shape[1]

    def puts(slot, down_ref, up_ref):
        return (
            pltpu.make_async_copy(down_ref, down_grad.at[slot], put.at[0, slot]),
            pltpu.make_async_copy(up_ref, up_grad.at[slot], put.at[1, slot]),
        )

    out_puts = (
        pltpu.make_async_copy(out_in, out, put_out.at[0]),
        pltpu.make_async_copy(tig_in, tig, put_out.at[1]),
    )

    for copy in out_puts:
        copy.start()
    no_down[...] = jnp.zeros_like(no_down)
    no_up[...] = jnp.zeros_like(no_up)

    @pl.loop(0, slots)
    def _(slot):
        @pl.when(start[slot] == start[slot + 1])
        def _():
            for copy in puts(slot, no_down, no_up):
                copy.start()

    @pl.loop(0, n)
    def _(i):
        k = order[i]
        slot = slot_map[block_adapter[k]]
        over_rows = (((0,), (0,)), ((), ()))
        term_a = lax.dot_general(
            x_slab[k], packs[k, rows:, :], over_rows, preferred_element_type=jnp.float32
        )
        term_b = lax.dot_general(
            packs[k, :rows, :], g_slab[k], over_rows, preferred_element_type=jnp.float32
        )
        fresh = i == start[slot]
        acc_a[...] = jnp.where(fresh, term_a, acc_a[...] + term_a)
        acc_b[...] = jnp.where(fresh, term_b, acc_b[...] + term_b)

        @pl.when(i + 1 == start[slot + 1])
        def _():
            held = jnp.maximum(counts[block_adapter[k]], 1)
            scale = 1.0 / jnp.full((1, 128), held, jnp.int32).astype(jnp.float32)
            sum_a[i] = (acc_a[...] * scale[:, :1]).astype(jnp.bfloat16)
            sum_b[i] = (adapter_scale * acc_b[...] * scale[:, :1]).astype(jnp.bfloat16)
            for copy in puts(slot, sum_a.at[i], sum_b.at[i]):
                copy.start()

    for copy in out_puts:
        copy.wait()

    @pl.loop(0, slots)
    def _(slot):
        for copy in puts(slot, no_down, no_up):
            copy.wait()


def factor_gradients(block_adapter, counts, slot_map, order, start, x_slab, g_slab, packs, out, tig):
    slots = slot_map.shape[0]
    n, rows, seg = x_slab.shape
    rank = packs.shape[2]
    hbm = pl.BlockSpec(memory_space=pltpu.HBM)
    vmem = pl.BlockSpec(memory_space=pltpu.VMEM)
    smem = pl.BlockSpec(memory_space=pltpu.SMEM)
    bf16, f32 = jnp.bfloat16, jnp.float32
    sems = pltpu.SemaphoreType.DMA
    return pl.pallas_call(
        functools.partial(factor_kernel, n, slots),
        in_specs=[smem] * 5 + [vmem] * 3 + [vmem] * 2,
        out_specs=[hbm] * 4,
        out_shape=[
            jax.ShapeDtypeStruct(out.shape, bf16),
            jax.ShapeDtypeStruct(tig.shape, bf16),
            jax.ShapeDtypeStruct((slots, seg, rank), bf16),
            jax.ShapeDtypeStruct((slots, rank, seg), bf16),
        ],
        scratch_shapes=[
            pltpu.VMEM((seg, rank), bf16),
            pltpu.VMEM((rank, seg), bf16),
            pltpu.VMEM((seg, rank), f32),
            pltpu.VMEM((rank, seg), f32),
            pltpu.VMEM((n, seg, rank), bf16),
            pltpu.VMEM((n, rank, seg), bf16),
            sems((2, slots)),
            sems((2,)),
        ],
        compiler_params=pltpu.CompilerParams(vmem_limit_bytes=24 * MIB),
        name="factor_gradients",
    )(block_adapter, counts, slot_map, order, start, x_slab, g_slab, packs, out, tig)


def kernel_body(tokens, grad_out, down_factor_pool, up_pool, *tables):
    n = lax.axis_size("dp")
    down_sel, up_sel, mask, order, start = pick(*tables, down_factor_pool, up_pool)
    out, tig, x_slab, g_slab, packs = exchange(n, tokens, grad_out, down_sel, up_sel, mask)
    return factor_gradients(*tables, order, start, x_slab, g_slab, packs, out, tig)


def body(tokens, *rest):
    n = lax.axis_size("dp")
    seg = rest[1].shape[1]
    if tokens.shape[0] == BLOCK and seg % 128 == 0 and n % 2 == 0:
        return kernel_body(tokens, *rest)
    return collective_body(tokens, *rest)


def solution(mesh):
    placed = (
        P(("group", "dp"), None),
        P(("group", "dp"), None),
        P("group", "dp", None),
        P("group", None, "dp"),
        P("group"),
        P("group"),
        P("group"),
    )
    return jax.shard_map(
        body,
        mesh=mesh,
        in_specs=placed,
        out_specs=(
            P(("group", "dp"), None),
            P(("group", "dp"), None),
            P("group", "dp", None),
            P("group", None, "dp"),
        ),
        check_vma=False,
    )
```
